512 devices in a mesh: head: 8 (over y_hi, x), ctx: 64 (over z, y_lo, core).
Axes of the slice: x: 4, y: 8 (y_hi: 2, y_lo: 4; y = y_hi * 4 + y_lo), z: 8, core: 2. Of those that a mesh axis runs over, the one named last changes fastest.
Arguments:
- queries: bfloat16 [32768, 8192], P(('head', 'ctx')), may hold values from -4.5 to 4.5
- key_tensor: bfloat16 [32768, 1024], P(('head', 'ctx')), may hold values from -4.5 to 4.5
- value_tensor: bfloat16 [32768, 1024], P(('head', 'ctx')), may hold values from -6 to 6
- positions: int32 [32768], P(('head', 'ctx')), may hold values from 0 to 32767, as said below
Outputs:
- attended: bfloat16 [32768, 8192], P(('head', 'ctx'))
The draws below stay inside these ranges and needn't reach their ends.
Inputs may be any that keep to these rules, and one draw needn't show every extreme that they name: A permutation of the positions. Take the rows held by one index c of ctx, in the order of the head indices: they are two whole blocks of 256 consecutive positions in increasing order, block k and block 127 - k for some k, in either order.
All inputs are finite; a program needn't handle non-finite values.
Results may differ from the reference program's by a relative error of at most 0.0045.
Values may be sent and summed in bfloat16 or wider, within the bound.
No kernel may reach another device: no remote copies, remote signals or barrier semaphores. Data moves between devices by JAX's collectives and lax.ppermute only.
A program may use at most 64 MiB of HBM per device.

```python
import math
import jax
import jax.numpy as jnp
from jax import lax

QUERY_HEADS = 64
KEY_VALUE_HEADS = 8
HEAD_DIMENSION = 128
TOKENS_PER_SHARD = 512
WINDOW_BLOCKS = 3
TOKEN_TOTAL = 32768
ROWS = 64
N_HEAD = 8
N_CTX = 64


def layout(key):
    half_rows = TOKENS_PER_SHARD // 2
    order = jax.random.permutation(jax.random.fold_in(key, 11), N_CTX).astype(jnp.int32)
    flips = jax.random.randint(jax.random.fold_in(key, 12), (N_CTX,), 0, 2)
    mirror = 2 * N_CTX - 1 - order
    first_block = jnp.where(flips == 1, mirror, order)
    second_block = jnp.where(flips == 1, order, mirror)
    offsets = jnp.arange(half_rows, dtype=jnp.int32)
    by_shard = jnp.concatenate([first_block[:, None] * half_rows + offsets[None, :], second_block[:, None] * half_rows + offsets[None, :]], axis=1)
    broadcast_heads = by_shard.reshape(N_CTX, N_HEAD, TOKENS_PER_SHARD // N_HEAD).transpose(1, 0, 2)
    return broadcast_heads.reshape(TOKEN_TOTAL).astype(jnp.int32)


def coarse_sample(key, width):
    value_entries = jax.random.normal(jax.random.fold_in(key, 3), (TOKEN_TOTAL, width)) * 1.4
    return jnp.clip(value_entries, -4.5, 4.5).astype(jnp.float32)


def draw_queries(key, part):
    value_entries = coarse_sample(jax.random.fold_in(key, 31), QUERY_HEADS * HEAD_DIMENSION)
    return value_entries.astype(jnp.bfloat16)


def draw_key_tensor(key, part):
    value_entries = coarse_sample(jax.random.fold_in(key, 41), KEY_VALUE_HEADS * HEAD_DIMENSION)
    return value_entries.astype(jnp.bfloat16)


def draw_positions(key, part):
    return layout(key)


def levels(stream_key, dims, cuts, least, top_value):
    factor_of, own = 1.0, jax.random.fold_in(stream_key, 6)
    for axis_at, parts in cuts:
        steps = jnp.exp(jax.random.uniform(jax.random.fold_in(own, axis_at), (parts,), jnp.float32, least / len(cuts), top_value / len(cuts)))
        factor_of = factor_of * jnp.repeat(steps, dims[axis_at] // parts).reshape([-1 if axis == axis_at else 1 for axis in range(len(dims))])
    return factor_of


def gaussian(rng, extent, spread, most, pieces=(), kind=jnp.bfloat16):
    entries = jax.random.normal(rng, extent, jnp.float32) * spread
    if len(pieces) > 0:
        entries = levels(rng, extent, pieces, -0.22, 0.18) * entries
    return jnp.clip(entries, min=-most, max=most).astype(kind)


def setup_inputs(seed: int = 0) -> dict:
    key_list = jax.random.split(jax.random.key(seed), 5)
    queries = draw_queries(jax.random.fold_in(key_list[4], 71), 0)
    key_tensor = draw_key_tensor(jax.random.fold_in(key_list[4], 71), 0)
    value_tensor = gaussian(key_list[2], (TOKEN_TOTAL, KEY_VALUE_HEADS * HEAD_DIMENSION), 1.0, 6.0, ((0, 512),))
    positions = draw_positions(jax.random.fold_in(key_list[4], 71), 0)
    return {"queries": queries, "key_tensor": key_tensor, "value_tensor": value_tensor, "positions": positions}


neg_big = -1e+30

def per_context_slot(array):
    rest = array.shape[1:]
    reshaped_tensor = array.reshape((N_HEAD, N_CTX, ROWS) + rest)
    reshaped_tensor = jnp.swapaxes(reshaped_tensor, 0, 1)
    return reshaped_tensor.reshape((N_CTX, TOKENS_PER_SHARD) + rest)

def reference(queries, key_tensor, value_tensor, positions):
    query_groups = QUERY_HEADS // KEY_VALUE_HEADS
    score_scale = 1.0 / math.sqrt(HEAD_DIMENSION)
    query_context = per_context_slot(queries).reshape(N_CTX, TOKENS_PER_SHARD, KEY_VALUE_HEADS, query_groups, HEAD_DIMENSION)
    key_context = per_context_slot(key_tensor).reshape(N_CTX, TOKENS_PER_SHARD, KEY_VALUE_HEADS, HEAD_DIMENSION)
    value_context = per_context_slot(value_tensor).reshape(N_CTX, TOKENS_PER_SHARD, KEY_VALUE_HEADS, HEAD_DIMENSION)
    p_ctx = per_context_slot(positions)
    query_block_index = min(TOKENS_PER_SHARD, 128)

    def one_ctx(shard_index):
        block_delays = (shard_index - jnp.arange(WINDOW_BLOCKS + 1, dtype=jnp.int32)) % N_CTX
        key_row_block = key_context[block_delays].reshape((WINDOW_BLOCKS + 1) * TOKENS_PER_SHARD, KEY_VALUE_HEADS, HEAD_DIMENSION).astype(jnp.float32)
        value_row_block = value_context[block_delays].reshape((WINDOW_BLOCKS + 1) * TOKENS_PER_SHARD, KEY_VALUE_HEADS, HEAD_DIMENSION).astype(jnp.float32)
        key_pos = p_ctx[block_delays].reshape((WINDOW_BLOCKS + 1) * TOKENS_PER_SHARD)
        query_resident = query_context[shard_index].reshape(TOKENS_PER_SHARD // query_block_index, query_block_index, KEY_VALUE_HEADS, query_groups, HEAD_DIMENSION)
        p_here = p_ctx[shard_index].reshape(TOKENS_PER_SHARD // query_block_index, query_block_index)

        def one_block(packed):
            q_part, pos_part = packed
            scores = jnp.einsum('skgd,tkd->skgt', q_part.astype(jnp.float32), key_row_block) * score_scale
            visible = (key_pos[None, :] <= pos_part[:, None])[:, None, None, :]
            scores = jnp.where(visible, scores, neg_big)
            maxima = lax.optimization_barrier(jnp.max(scores, axis=-1, keepdims=True))
            weights = jnp.where(visible, jnp.exp(scores - maxima), 0.0)
            denominator = lax.optimization_barrier(jnp.sum(weights, axis=-1))
            rounded = lax.optimization_barrier(weights.astype(jnp.bfloat16))
            summed = jnp.einsum('skgt,tkd->skgd', rounded.astype(jnp.float32), value_row_block)
            return (summed / denominator[..., None]).astype(jnp.bfloat16)
        return lax.map(one_block, (query_resident, p_here)).reshape(TOKENS_PER_SHARD, QUERY_HEADS * HEAD_DIMENSION)
    result = lax.map(one_ctx, jnp.arange(N_CTX, dtype=jnp.int32))
    result = jnp.swapaxes(result.reshape(N_CTX, N_HEAD, ROWS, QUERY_HEADS * HEAD_DIMENSION), 0, 1)
    return result.reshape(TOKEN_TOTAL, QUERY_HEADS * HEAD_DIMENSION)
```

```python
import math

import jax
import jax.numpy as jnp
from jax import lax
from jax.experimental import pallas as pl
from jax.experimental.pallas import tpu as pltpu
from jax.sharding import Mesh
from jax.sharding import PartitionSpec as P

HEAD_DIMENSION = 128
RUN = 256
ROWS = 64
FLAG_ROWS = 8
GROUP = 8
SCALE = math.log2(math.e) / math.sqrt(HEAD_DIMENSION)
NEG_BIG = -1e30
AXES = ("yh", "x", "z", "yl", "c")
SIZES = (2, 4, 8, 4, 2)
MIB = 1024 * 1024


def ring_route(shift, back):
    nyh, nx, nz, nyl, nc = SIZES
    route = []
    for yh in range(nyh):
        for x in range(nx):
            for z in range(nz):
                for yl in range(nyl):
                    for c in range(nc):
                        ring = (yh * nyl + yl - shift) % (nyh * nyl)
                        chain = (z * nyl + yl - back) % (nz * nyl)
                        z2, yl2 = divmod(chain, nyl)
                        src = (((ring // nyl * nx + x) * nz + z2) * nyl + yl2) * nc + c
                        dst = (((yh * nx + x) * nz + z) * nyl + yl) * nc + c
                        route.append((src, dst))
    return route


def vmem(count):
    return [pl.BlockSpec(memory_space=pltpu.VMEM)] * count


def smem():
    return [pl.BlockSpec(memory_space=pltpu.SMEM)]


def pack_kernel(pos_ref, k_ref, v_ref, out_ref):
    run = jnp.right_shift(pos_ref[0], 8).astype(jnp.float32)
    flags = jnp.full((FLAG_ROWS, 256), run, jnp.float32).astype(jnp.bfloat16)
    for g in range(8):
        lanes = slice(g * 128, (g + 1) * 128)
        both = jnp.concatenate([k_ref[:, lanes], v_ref[:, lanes]], axis=1)
        out_ref[g] = jnp.concatenate([both, flags], axis=0)


def pack(positions, key_tensor, value_tensor):
    return pl.pallas_call(
        pack_kernel,
        out_shape=jax.ShapeDtypeStruct((8, ROWS + FLAG_ROWS, 256), jnp.bfloat16),
        in_specs=smem() + vmem(2),
        out_specs=vmem(1)[0],
        compiler_params=pltpu.CompilerParams(vmem_limit_bytes=56 * MIB),
    )(positions, key_tensor, value_tensor)


def repack_kernel(in_ref, out_ref):
    flags = []
    for c in range(2):
        for x in range(4):
            block = in_ref[c * 4 + x]
            at = c * RUN + x * ROWS
            out_ref[at : at + ROWS, :] = block[0:ROWS, :]
        flags.append(block[ROWS : ROWS + FLAG_ROWS, 0:128])
    line = jnp.concatenate(flags, axis=1)
    out_ref[2 * RUN : 2 * RUN + 16, :] = jnp.concatenate([line, line], axis=0)


def relay_kernel(own_ref, other_ref, out_ref):
    last = slice(2 * RUN, 2 * RUN + 16)
    out_ref[0:RUN, :] = own_ref[RUN : 2 * RUN, :]
    out_ref[RUN : 2 * RUN, :] = other_ref[RUN : 2 * RUN, :]
    out_ref[last, 0:128] = own_ref[last, 128:256]
    out_ref[last, 128:256] = other_ref[last, 128:256]


def rearrange(kernel, *operands):
    return pl.pallas_call(
        kernel,
        out_shape=jax.ShapeDtypeStruct((2 * RUN + 16, 256), jnp.bfloat16),
        in_specs=vmem(len(operands)),
        out_specs=vmem(1)[0],
        compiler_params=pltpu.CompilerParams(vmem_limit_bytes=4 * MIB),
    )(*operands)


def flag(ref, half):
    tile = ref[2 * RUN : 2 * RUN + 16, half * 128 : (half + 1) * 128].astype(jnp.float32)
    return jnp.max(tile).astype(jnp.int32)


def blocks(ref):
    return [(ref, 0, flag(ref, 0)), (ref, RUN, flag(ref, 1))]


def gather_visible(slots, own_run, kv_ref, start):
    count = jnp.int32(start)
    for ref, row, run in slots:
        seen = run < own_run
        at = count

        @pl.when(seen)
        def _(ref=ref, row=row, at=at):
            kv_ref[at] = ref[row : row + RUN, :]

        count = count + seen.astype(jnp.int32)
    return count


def scores_of(q_ref, i, h, keys):
    q = q_ref[i * RUN : (i + 1) * RUN, h * 128 : (h + 1) * 128]
    return lax.dot_general(q, keys, (((1,), (1,)), ((), ())), preferred_element_type=jnp.float32)


def lane_fold(s):
    return jnp.maximum(s[:, 0:128], s[:, 128:256])


def add_values(s_ref, m_ref, acc_ref, kv_ref, i, j):
    values = jnp.concatenate([kv_ref[j, :, 128:256], jnp.ones((RUN, 128), jnp.bfloat16)], axis=1)
    for h in range(GROUP):
        m = m_ref[i, h]
        s = s_ref[j, h]
        weights = jnp.concatenate(
            [jnp.exp2((s[:, 0:128] - m) * SCALE), jnp.exp2((s[:, 128:256] - m) * SCALE)], axis=1
        )
        part = jnp.dot(weights.astype(jnp.bfloat16), values, preferred_element_type=jnp.float32)
        acc_ref[i, h] = acc_ref[i, h] + part


def first_kernel(q_ref, own_ref, p1_ref, p2_ref, m_ref, acc_ref, kv_ref, s_ref):
    own, other, behind = blocks(own_ref), blocks(p1_ref), blocks(p2_ref)
    slots = [[other[0]] + behind, [other[1], own[0], other[0]] + behind]
    lower = lax.broadcasted_iota(jnp.int32, (RUN, RUN), 0) >= lax.broadcasted_iota(
        jnp.int32, (RUN, RUN), 1
    )
    for i in range(2):
        kv_ref[0] = own_ref[i * RUN : (i + 1) * RUN, :]
        count = gather_visible(slots[i], own[i][2], kv_ref, 1)
        keys = kv_ref[0, :, 0:128]
        for h in range(GROUP):
            s = jnp.where(lower, scores_of(q_ref, i, h, keys), NEG_BIG)
            s_ref[0, h] = s
            m_ref[i, h] = lane_fold(s)

        @pl.loop(1, count)
        def _(j):
            keys = kv_ref[j, :, 0:128]
            for h in range(GROUP):
                s = scores_of(q_ref, i, h, keys)
                s_ref[j, h] = s
                m_ref[i, h] = jnp.maximum(m_ref[i, h], lane_fold(s))

        for h in range(GROUP):
            m_ref[i, h] = jnp.broadcast_to(jnp.max(m_ref[i, h], axis=1, keepdims=True), (RUN, 128))
            acc_ref[i, h] = jnp.zeros((RUN, 256), jnp.float32)

        @pl.loop(0, count)
        def _(j):
            add_values(s_ref, m_ref, acc_ref, kv_ref, i, j)


def second_kernel(
    q_ref, own_ref, p3_ref, p4_ref, m1_ref, acc1_ref, out_ref, m_ref, acc_ref, kv_ref, s_ref
):
    own, behind = blocks(own_ref), blocks(p4_ref)
    slots = [behind + blocks(p3_ref), behind]
    for i in range(2):
        count = gather_visible(slots[i], own[i][2], kv_ref, 0)
        for h in range(GROUP):
            m_ref[i, h] = m1_ref[i, h]

        @pl.loop(0, count)
        def _(j):
            keys = kv_ref[j, :, 0:128]
            for h in range(GROUP):
                s = scores_of(q_ref, i, h, keys)
                s_ref[j, h] = s
                m_ref[i, h] = jnp.maximum(m_ref[i, h], lane_fold(s))

        for h in range(GROUP):
            m = jnp.broadcast_to(jnp.max(m_ref[i, h], axis=1, keepdims=True), (RUN, 128))
            m_ref[i, h] = m
            rescale = jnp.exp2((m1_ref[i, h] - m) * SCALE)
            acc_ref[i, h, :, 0:128] = acc1_ref[i, h, :, 0:128] * rescale
            acc_ref[i, h, :, 128:256] = acc1_ref[i, h, :, 128:256] * rescale

        @pl.loop(0, count)
        def _(j):
            add_values(s_ref, m_ref, acc_ref, kv_ref, i, j)

        for h in range(GROUP):
            out_ref[i * RUN : (i + 1) * RUN, h * 128 : (h + 1) * 128] = (
                acc_ref[i, h, :, 0:128] / acc_ref[i, h, :, 128:256]
            ).astype(jnp.bfloat16)


MAX_SHAPE = (2, GROUP, RUN, 128)
ACC_SHAPE = (2, GROUP, RUN, 256)


def first_part(*operands):
    return pl.pallas_call(
        first_kernel,
        out_shape=(
            jax.ShapeDtypeStruct(MAX_SHAPE, jnp.float32),
            jax.ShapeDtypeStruct(ACC_SHAPE, jnp.float32),
        ),
        in_specs=vmem(4),
        out_specs=tuple(vmem(2)),
        scratch_shapes=[
            pltpu.VMEM((6, RUN, 256), jnp.bfloat16),
            pltpu.VMEM((6, GROUP, RUN, 256), jnp.float32),
        ],
        compiler_params=pltpu.CompilerParams(vmem_limit_bytes=24 * MIB),
        cost_estimate=pl.CostEstimate(flops=8 << 29, bytes_accessed=8 << 20, transcendentals=4 << 20),
    )(*operands)


def second_part(*operands):
    return pl.pallas_call(
        second_kernel,
        out_shape=jax.ShapeDtypeStruct((2 * RUN, GROUP * 128), jnp.bfloat16),
        in_specs=vmem(6),
        out_specs=vmem(1)[0],
        scratch_shapes=[
            pltpu.VMEM(MAX_SHAPE, jnp.float32),
            pltpu.VMEM(ACC_SHAPE, jnp.float32),
            pltpu.VMEM((4, RUN, 256), jnp.bfloat16),
            pltpu.VMEM((4, GROUP, RUN, 256), jnp.float32),
        ],
        compiler_params=pltpu.CompilerParams(vmem_limit_bytes=24 * MIB),
        cost_estimate=pl.CostEstimate(flops=4 << 29, bytes_accessed=8 << 20, transcendentals=2 << 20),
    )(*operands)


def body(queries, key_tensor, value_tensor, positions):
    group = ("c", "x")
    packed = pack(positions, key_tensor, value_tensor)
    own = rearrange(
        repack_kernel, lax.all_to_all(packed, group, split_axis=0, concat_axis=0, tiled=True)
    )
    p1 = lax.ppermute(own, AXES, ring_route(4, 0))
    p2 = lax.ppermute(own, AXES, ring_route(1, 1))
    p4 = lax.ppermute(own, AXES, ring_route(5, 1))
    p3 = lax.ppermute(rearrange(relay_kernel, own, p1), AXES, ring_route(2, 2))
    q = lax.all_to_all(
        queries.reshape(ROWS, 8, GROUP * 128), group, split_axis=1, concat_axis=0, tiled=True
    ).reshape(2 * RUN, GROUP * 128)
    m1, acc1 = first_part(q, own, p1, p2)
    out = second_part(q, own, p3, p4, m1, acc1)
    result = lax.all_to_all(
        out.reshape(8, ROWS, GROUP * 128), group, split_axis=0, concat_axis=2, tiled=True
    )
    return result.reshape(ROWS, 8 * GROUP * 128)


def solution(mesh):
    finer = Mesh(mesh.devices.reshape(SIZES), AXES)
    return jax.shard_map(
        body,
        mesh=finer,
        in_specs=(P(AXES, None), P(AXES, None), P(AXES, None), P(AXES)),
        out_specs=P(AXES, None),
        check_vma=False,
    )
```

```python
import math

import jax
import jax.numpy as jnp
from jax import lax
from jax.experimental import pallas as pl
from jax.experimental.pallas import tpu as pltpu
from jax.sharding import Mesh
from jax.sharding import PartitionSpec as P

HEAD_DIMENSION = 128
RUN = 256
ROWS = 64
FLAG_ROWS = 8
GROUP = 8
SCALE = math.log2(math.e) / math.sqrt(HEAD_DIMENSION)
NEG_BIG = -1e30
AXES = ("yh", "x", "z", "yl", "c")
SIZES = (2, 4, 8, 4, 2)
MIB = 1024 * 1024


def ring_route(shift, back):
    nyh, nx, nz, nyl, nc = SIZES
    route = []
    for yh in range(nyh):
        for x in range(nx):
            for z in range(nz):
                for yl in range(nyl):
                    for c in range(nc):
                        ring = (yh * nyl + yl - shift) % (nyh * nyl)
                        chain = (z * nyl + yl - back) % (nz * nyl)
                        z2, yl2 = divmod(chain, nyl)
                        src = (((ring // nyl * nx + x) * nz + z2) * nyl + yl2) * nc + c
                        dst = (((yh * nx + x) * nz + z) * nyl + yl) * nc + c
                        route.append((src, dst))
    return route


def vmem(count):
    return [pl.BlockSpec(memory_space=pltpu.VMEM)] * count


def smem():
    return [pl.BlockSpec(memory_space=pltpu.SMEM)]


def pack_kernel(pos_ref, k_ref, v_ref, out_ref):
    run = jnp.right_shift(pos_ref[0], 8).astype(jnp.float32)
    flags = jnp.full((FLAG_ROWS, 256), run, jnp.float32).astype(jnp.bfloat16)
    for g in range(8):
        lanes = slice(g * 128, (g + 1) * 128)
        both = jnp.concatenate([k_ref[:, lanes], v_ref[:, lanes]], axis=1)
        out_ref[g] = jnp.concatenate([both, flags], axis=0)


def pack(positions, key_tensor, value_tensor):
    return pl.pallas_call(
        pack_kernel,
        out_shape=jax.ShapeDtypeStruct((8, ROWS + FLAG_ROWS, 256), jnp.bfloat16),
        in_specs=smem() + vmem(2),
        out_specs=vmem(1)[0],
        compiler_params=pltpu.CompilerParams(vmem_limit_bytes=56 * MIB),
    )(positions, key_tensor, value_tensor)


def repack_kernel(in_ref, out_ref):
    flags = []
    for c in range(2):
        for x in range(4):
            block = in_ref[c * 4 + x]
            at = c * RUN + x * ROWS
            out_ref[at : at + ROWS, :] = block[0:ROWS, :]
        flags.append(block[ROWS : ROWS + FLAG_ROWS, 0:128])
    line = jnp.concatenate(flags, axis=1)
    out_ref[2 * RUN : 2 * RUN + 16, :] = jnp.concatenate([line, line], axis=0)


def relay_kernel(own_ref, other_ref, out_ref):
    last = slice(2 * RUN, 2 * RUN + 16)
    out_ref[0:RUN, :] = own_ref[RUN : 2 * RUN, :]
    out_ref[RUN : 2 * RUN, :] = other_ref[RUN : 2 * RUN, :]
    out_ref[last, 0:128] = own_ref[last, 128:256]
    out_ref[last, 128:256] = other_ref[last, 128:256]


def rearrange(kernel, *operands):
    return pl.pallas_call(
        kernel,
        out_shape=jax.ShapeDtypeStruct((2 * RUN + 16, 256), jnp.bfloat16),
        in_specs=vmem(len(operands)),
        out_specs=vmem(1)[0],
        compiler_params=pltpu.CompilerParams(vmem_limit_bytes=4 * MIB),
    )(*operands)


def flag(ref, half):
    rows = ref.shape[0]
    tile = ref[rows - 16 : rows, half * 128 : (half + 1) * 128].astype(jnp.float32)
    return jnp.max(tile).astype(jnp.int32)


def gather_visible(slots, own_run, kv_ref, i, start):
    count = jnp.int32(start)
    for ref, row, run in slots:
        seen = run < own_run
        at = count

        @pl.when(seen)
        def _(ref=ref, row=row, at=at):
            kv_ref[i, at] = ref[row : row + RUN, :]

        count = count + seen.astype(jnp.int32)
    return count


def lane_fold(s):
    return jnp.maximum(s[:, 0:128], s[:, 128:256])


def scores(q, keys):
    return lax.dot_general(q, keys, (((1,), (1,)), ((), ())), preferred_element_type=jnp.float32)


def queries_of(q_ref, i, h):
    return q_ref[pl.ds(pl.multiple_of(i * RUN, RUN), RUN), h * 128 : (h + 1) * 128]


def head_rows(h):
    return slice(h * RUN, (h + 1) * RUN)


def weighted(s_ref, m_ref, kv_ref, i, at, rows):
    m = m_ref[i, rows, :]
    weights, values = [], []
    for j in at:
        for lanes in (slice(0, 128), slice(128, 256)):
            weights.append(jnp.exp2((s_ref[j, rows, lanes] - m) * SCALE).astype(jnp.bfloat16))
        values.append(kv_ref[i, j, :, 128:256])
    values = jnp.concatenate(values, axis=0)
    values = jnp.concatenate([values, jnp.ones(values.shape, jnp.bfloat16)], axis=1)
    return jnp.dot(jnp.concatenate(weights, axis=1), values, preferred_element_type=jnp.float32)


def row_max(m):
    return jnp.broadcast_to(jnp.max(m, axis=1, keepdims=True), m.shape)


def first_kernel(q_ref, own_ref, other_ref, p2_ref, m_ref, acc_ref, kv_ref, s_ref):
    runs = [flag(own_ref, c) for c in range(2)]
    other = [(other_ref, c * RUN, 127 - runs[c]) for c in range(2)]
    near = [(p2_ref, c * RUN, flag(p2_ref, c)) for c in range(2)]
    slots = [[other[0]] + near, [other[1], (own_ref, 0, runs[0]), other[0]] + near]
    counts = []
    for i in range(2):
        kv_ref[i, 0] = own_ref[i * RUN : (i + 1) * RUN, :]
        counts.append(gather_visible(slots[i], runs[i], kv_ref, i, 1))
    lower = lax.broadcasted_iota(jnp.int32, (RUN, RUN), 0) >= lax.broadcasted_iota(
        jnp.int32, (RUN, RUN), 1
    )

    @pl.loop(0, 2)
    def _(i):
        count = jnp.where(i == 0, counts[0], counts[1])
        for h in range(GROUP):
            s = jnp.where(lower, scores(queries_of(q_ref, i, h), kv_ref[i, 0, :, 0:128]), NEG_BIG)
            s_ref[0, head_rows(h), :] = s
            m_ref[i, head_rows(h), :] = lane_fold(s)

        @pl.loop(1, count)
        def _(j):
            for h in range(GROUP):
                s = scores(queries_of(q_ref, i, h), kv_ref[i, j, :, 0:128])
                s_ref[j, head_rows(h), :] = s
                m_ref[i, head_rows(h), :] = jnp.maximum(m_ref[i, head_rows(h), :], lane_fold(s))

        for h in range(GROUP):
            m_ref[i, head_rows(h), :] = row_max(m_ref[i, head_rows(h), :])
            acc_ref[i, head_rows(h), :] = weighted(s_ref, m_ref, kv_ref, i, [0], head_rows(h))

        @pl.loop(1, count)
        def _(j):
            for h in range(GROUP):
                acc_ref[i, head_rows(h), :] = acc_ref[i, head_rows(h), :] + weighted(
                    s_ref, m_ref, kv_ref, i, [j], head_rows(h)
                )


def second_kernel(
    q_ref, own_ref, p4_ref, p3_ref, m1_ref, acc1_ref, out_ref, m_ref, acc_ref, kv_ref, s_ref
):
    runs = [flag(own_ref, c) for c in range(2)]
    near = [(p4_ref, c * RUN, flag(p4_ref, c)) for c in range(2)]
    far = [(p3_ref, c * RUN, flag(p3_ref, c)) for c in range(2)]
    slots = [near + far, near]
    counts = [gather_visible(slots[i], runs[i], kv_ref, i, 0) for i in range(2)]

    @pl.loop(0, 2)
    def _(i):
        count = jnp.where(i == 0, counts[0], counts[1])
        for h in range(GROUP):
            m_ref[i, head_rows(h), :] = m1_ref[i, head_rows(h), :]

        @pl.loop(0, count)
        def _(j):
            for h in range(GROUP):
                s = scores(queries_of(q_ref, i, h), kv_ref[i, j, :, 0:128])
                s_ref[j, head_rows(h), :] = s
                m_ref[i, head_rows(h), :] = jnp.maximum(m_ref[i, head_rows(h), :], lane_fold(s))

        for h in range(GROUP):
            m = row_max(m_ref[i, head_rows(h), :])
            m_ref[i, head_rows(h), :] = m
            rescale = jnp.exp2((m1_ref[i, head_rows(h), :] - m) * SCALE)
            for lanes in (slice(0, 128), slice(128, 256)):
                acc_ref[head_rows(h), lanes] = acc1_ref[i, head_rows(h), lanes] * rescale
        odd = count % 2

        @pl.when(odd == 1)
        def _():
            for h in range(GROUP):
                acc_ref[head_rows(h), :] = acc_ref[head_rows(h), :] + weighted(
                    s_ref, m_ref, kv_ref, i, [0], head_rows(h)
                )

        @pl.loop(0, count // 2)
        def _(pair):
            j = odd + 2 * pair
            for h in range(GROUP):
                acc_ref[head_rows(h), :] = acc_ref[head_rows(h), :] + weighted(
                    s_ref, m_ref, kv_ref, i, [j, j + 1], head_rows(h)
                )

        at = pl.ds(pl.multiple_of(i * RUN, RUN), RUN)
        for h in range(GROUP):
            block = acc_ref[head_rows(h), :]
            out_ref[at, h * 128 : (h + 1) * 128] = (block[:, 0:128] / block[:, 128:256]).astype(
                jnp.bfloat16
            )


def first_part(*operands):
    return pl.pallas_call(
        first_kernel,
        out_shape=(
            jax.ShapeDtypeStruct((2, GROUP * RUN, 128), jnp.float32),
            jax.ShapeDtypeStruct((2, GROUP * RUN, 256), jnp.float32),
        ),
        in_specs=vmem(4),
        out_specs=tuple(vmem(2)),
        scratch_shapes=[
            pltpu.VMEM((2, 6, RUN, 256), jnp.bfloat16),
            pltpu.VMEM((6, GROUP * RUN, 256), jnp.float32),
        ],
        compiler_params=pltpu.CompilerParams(vmem_limit_bytes=20 * MIB),
        cost_estimate=pl.CostEstimate(flops=4 << 29, bytes_accessed=8 << 20, transcendentals=2 << 20),
    )(*operands)


def second_part(*operands):
    return pl.pallas_call(
        second_kernel,
        out_shape=jax.ShapeDtypeStruct((2 * RUN, GROUP * 128), jnp.bfloat16),
        in_specs=vmem(6),
        out_specs=vmem(1)[0],
        scratch_shapes=[
            pltpu.VMEM((2, GROUP * RUN, 128), jnp.float32),
            pltpu.VMEM((GROUP * RUN, 256), jnp.float32),
            pltpu.VMEM((2, 4, RUN, 256), jnp.bfloat16),
            pltpu.VMEM((4, GROUP * RUN, 256), jnp.float32),
        ],
        compiler_params=pltpu.CompilerParams(vmem_limit_bytes=22 * MIB),
        cost_estimate=pl.CostEstimate(flops=4 << 29, bytes_accessed=8 << 20, transcendentals=2 << 20),
    )(*operands)


def body(queries, key_tensor, value_tensor, positions):
    group = ("c", "x")
    packed = pack(positions, key_tensor, value_tensor)
    own = rearrange(
        repack_kernel, lax.all_to_all(packed, group, split_axis=0, concat_axis=0, tiled=True)
    )
    p1 = lax.ppermute(own, AXES, ring_route(4, 0))
    p4 = lax.ppermute(own, AXES, ring_route(5, 1))
    p2 = lax.ppermute(own, AXES, ring_route(1, 1))
    p3 = lax.ppermute(rearrange(relay_kernel, own, p1), AXES, ring_route(2, 2))
    q = lax.all_to_all(
        queries.reshape(ROWS, 8, GROUP * 128), group, split_axis=1, concat_axis=0, tiled=True
    ).reshape(2 * RUN, GROUP * 128)
    m1, acc1 = first_part(q, own, p1, p2)
    out = second_part(q, own, p4, p3, m1, acc1)
    result = lax.all_to_all(
        out.reshape(8, ROWS, GROUP * 128), group, split_axis=0, concat_axis=2, tiled=True
    )
    return result.reshape(ROWS, 8 * GROUP * 128)


def solution(mesh):
    finer = Mesh(mesh.devices.reshape(SIZES), AXES)
    return jax.shard_map(
        body,
        mesh=finer,
        in_specs=(P(AXES, None), P(AXES, None), P(AXES, None), P(AXES)),
        out_specs=P(AXES, None),
        check_vma=False,
    )
```

```python
import functools
import math

import jax
import jax.numpy as jnp
from jax import lax
from jax.experimental import pallas as pl
from jax.experimental.pallas import tpu as pltpu
from jax.sharding import Mesh
from jax.sharding import PartitionSpec as P

HEAD_DIMENSION = 128
RUN = 256
ROWS = 64
FLAG_ROWS = 8
GROUP = 8
SCALE = math.log2(math.e) / math.sqrt(HEAD_DIMENSION)
NEG_BIG = -1e30
AXES = ("yh", "x", "z", "yl", "c")
SIZES = (2, 4, 8, 4, 2)
MIB = 1024 * 1024


def ring_route(shift, back):
    nyh, nx, nz, nyl, nc = SIZES
    route = []
    for yh in range(nyh):
        for x in range(nx):
            for z in range(nz):
                for yl in range(nyl):
                    for c in range(nc):
                        ring = (yh * nyl + yl - shift) % (nyh * nyl)
                        chain = (z * nyl + yl - back) % (nz * nyl)
                        z2, yl2 = divmod(chain, nyl)
                        src = (((ring // nyl * nx + x) * nz + z2) * nyl + yl2) * nc + c
                        dst = (((yh * nx + x) * nz + z) * nyl + yl) * nc + c
                        route.append((src, dst))
    return route


def vmem(count):
    return [pl.BlockSpec(memory_space=pltpu.VMEM)] * count


def smem():
    return [pl.BlockSpec(memory_space=pltpu.SMEM)]


def pack_kernel(pos_ref, k_ref, v_ref, out_ref):
    run = jnp.right_shift(pos_ref[0], 8).astype(jnp.float32)
    flags = jnp.full((FLAG_ROWS, 256), run, jnp.float32).astype(jnp.bfloat16)
    for g in range(8):
        lanes = slice(g * 128, (g + 1) * 128)
        both = jnp.concatenate([k_ref[:, lanes], v_ref[:, lanes]], axis=1)
        out_ref[g] = jnp.concatenate([both, flags], axis=0)


def pack(positions, key_tensor, value_tensor):
    return pl.pallas_call(
        pack_kernel,
        out_shape=jax.ShapeDtypeStruct((8, ROWS + FLAG_ROWS, 256), jnp.bfloat16),
        in_specs=smem() + vmem(2),
        out_specs=vmem(1)[0],
        compiler_params=pltpu.CompilerParams(vmem_limit_bytes=56 * MIB),
    )(positions, key_tensor, value_tensor)


def repack_kernel(in_ref, out_ref):
    flags = []
    for c in range(2):
        for x in range(4):
            block = in_ref[x * 2 + c]
            at = c * RUN + x * ROWS
            out_ref[at : at + ROWS, :] = block[0:ROWS, :]
        flags.append(block[ROWS : ROWS + FLAG_ROWS, 0:128])
    line = jnp.concatenate(flags, axis=1)
    out_ref[2 * RUN : 2 * RUN + 16, :] = jnp.concatenate([line, line], axis=0)


def relay_kernel(own_ref, other_ref, out_ref):
    last = slice(2 * RUN, 2 * RUN + 16)
    out_ref[0:RUN, :] = own_ref[RUN : 2 * RUN, :]
    out_ref[RUN : 2 * RUN, :] = other_ref[RUN : 2 * RUN, :]
    out_ref[last, 0:128] = own_ref[last, 128:256]
    out_ref[last, 128:256] = other_ref[last, 128:256]


def rearrange(kernel, *operands):
    return pl.pallas_call(
        kernel,
        out_shape=jax.ShapeDtypeStruct((2 * RUN + 16, 256), jnp.bfloat16),
        in_specs=vmem(len(operands)),
        out_specs=vmem(1)[0],
        compiler_params=pltpu.CompilerParams(vmem_limit_bytes=4 * MIB),
    )(*operands)


def flag(ref, half):
    rows = ref.shape[0]
    tile = ref[rows - 16 : rows, half * 128 : (half + 1) * 128].astype(jnp.float32)
    return jnp.max(tile).astype(jnp.int32)


def gather_visible(slots, own_run, kv_ref, i, start):
    count = jnp.int32(start)
    for ref, row, run in slots:
        seen = run < own_run
        at = count

        @pl.when(seen)
        def _(ref=ref, row=row, at=at):
            kv_ref[i, at] = ref[row : row + RUN, :]

        count = count + seen.astype(jnp.int32)
    return count


def lane_fold(s):
    return jnp.maximum(s[:, 0:128], s[:, 128:256])


def scores(q, keys):
    return lax.dot_general(q, keys, (((1,), (1,)), ((), ())), preferred_element_type=jnp.float32)


def queries_of(q_ref, i, h):
    return q_ref[:, i, :, h * 128 : (h + 1) * 128].reshape(RUN, 128)


def head_rows(h):
    return slice(h * RUN, (h + 1) * RUN)


def weighted(s_ref, m_ref, kv_ref, i, at, rows):
    m = m_ref[i, rows, :]
    weights, values = [], []
    for j in at:
        for lanes in (slice(0, 128), slice(128, 256)):
            weights.append(jnp.exp2((s_ref[j, rows, lanes] - m) * SCALE).astype(jnp.bfloat16))
        values.append(kv_ref[i, j, :, 128:256])
    values = jnp.concatenate(values, axis=0)
    values = jnp.concatenate([values, jnp.ones(values.shape, jnp.bfloat16)], axis=1)
    return jnp.dot(jnp.concatenate(weights, axis=1), values, preferred_element_type=jnp.float32)


def row_max(m):
    return jnp.broadcast_to(jnp.max(m, axis=1, keepdims=True), m.shape)


def first_kernel(q_ref, own_ref, other_ref, p2_ref, m_ref, acc_ref, kv_ref, s_ref):
    runs = [flag(own_ref, c) for c in range(2)]
    other = [(other_ref, c * RUN, 127 - runs[c]) for c in range(2)]
    near = [(p2_ref, c * RUN, flag(p2_ref, c)) for c in range(2)]
    slots = [[other[0]] + near, [other[1], (own_ref, 0, runs[0]), other[0]] + near]
    counts = []
    for i in range(2):
        kv_ref[i, 0] = own_ref[i * RUN : (i + 1) * RUN, :]
        counts.append(gather_visible(slots[i], runs[i], kv_ref, i, 1))
    lower = lax.broadcasted_iota(jnp.int32, (RUN, RUN), 0) >= lax.broadcasted_iota(
        jnp.int32, (RUN, RUN), 1
    )

    @pl.loop(0, 2)
    def _(i):
        count = jnp.where(i == 0, counts[0], counts[1])
        for h in range(GROUP):
            s = jnp.where(lower, scores(queries_of(q_ref, i, h), kv_ref[i, 0, :, 0:128]), NEG_BIG)
            s_ref[0, head_rows(h), :] = s
            m_ref[i, head_rows(h), :] = lane_fold(s)

        @pl.loop(1, count)
        def _(j):
            for h in range(GROUP):
                s = scores(queries_of(q_ref, i, h), kv_ref[i, j, :, 0:128])
                s_ref[j, head_rows(h), :] = s
                m_ref[i, head_rows(h), :] = jnp.maximum(m_ref[i, head_rows(h), :], lane_fold(s))

        for h in range(GROUP):
            m_ref[i, head_rows(h), :] = row_max(m_ref[i, head_rows(h), :])
            acc_ref[i, head_rows(h), :] = weighted(s_ref, m_ref, kv_ref, i, [0], head_rows(h))

        @pl.loop(1, count)
        def _(j):
            for h in range(GROUP):
                acc_ref[i, head_rows(h), :] = acc_ref[i, head_rows(h), :] + weighted(
                    s_ref, m_ref, kv_ref, i, [j], head_rows(h)
                )


def second_kernel(
    mine, core_ref, q_ref, own_ref, p4_ref, p3_ref, m1_ref, acc1_ref, out_ref, m_ref, acc_ref, kv_ref, s_ref
):
    i = core_ref[0] if mine else 1 - core_ref[0]
    own_run = jnp.where(i == 0, flag(own_ref, 0), flag(own_ref, 1))
    near = [(p4_ref, c * RUN, flag(p4_ref, c)) for c in range(2)]
    far = [(p3_ref, c * RUN, jnp.where(i == 0, flag(p3_ref, c), 128)) for c in range(2)]
    count = gather_visible(near + far, own_run, kv_ref, 0, 0)
    for h in range(GROUP):
        m_ref[0, head_rows(h), :] = m1_ref[i, head_rows(h), :]

    @pl.loop(0, count)
    def _(j):
        for h in range(GROUP):
            s = scores(queries_of(q_ref, i, h), kv_ref[0, j, :, 0:128])
            s_ref[j, head_rows(h), :] = s
            m_ref[0, head_rows(h), :] = jnp.maximum(m_ref[0, head_rows(h), :], lane_fold(s))

    for h in range(GROUP):
        m = row_max(m_ref[0, head_rows(h), :])
        m_ref[0, head_rows(h), :] = m
        rescale = jnp.exp2((m1_ref[i, head_rows(h), :] - m) * SCALE)
        for lanes in (slice(0, 128), slice(128, 256)):
            acc_ref[head_rows(h), lanes] = acc1_ref[i, head_rows(h), lanes] * rescale
    odd = count % 2

    @pl.when(odd == 1)
    def _():
        for h in range(GROUP):
            acc_ref[head_rows(h), :] = acc_ref[head_rows(h), :] + weighted(
                s_ref, m_ref, kv_ref, 0, [0], head_rows(h)
            )

    @pl.loop(0, count // 2)
    def _(pair):
        j = odd + 2 * pair
        for h in range(GROUP):
            acc_ref[head_rows(h), :] = acc_ref[head_rows(h), :] + weighted(
                s_ref, m_ref, kv_ref, 0, [j, j + 1], head_rows(h)
            )

    for h in range(GROUP):
        block = acc_ref[head_rows(h), :]
        out_ref[:, h * 128 : (h + 1) * 128] = (block[:, 0:128] / block[:, 128:256]).astype(
            jnp.bfloat16
        )


def join_kernel(core_ref, mine_ref, theirs_ref, out_ref):
    @pl.when(core_ref[0] == 0)
    def _():
        out_ref[:, 0 : GROUP * 128] = mine_ref[...]
        out_ref[:, GROUP * 128 : 2 * GROUP * 128] = theirs_ref[...]

    @pl.when(core_ref[0] == 1)
    def _():
        out_ref[:, 0 : GROUP * 128] = theirs_ref[...]
        out_ref[:, GROUP * 128 : 2 * GROUP * 128] = mine_ref[...]


def join(core, mine, theirs):
    return pl.pallas_call(
        join_kernel,
        out_shape=jax.ShapeDtypeStruct((RUN, 2 * GROUP * 128), jnp.bfloat16),
        in_specs=smem() + vmem(2),
        out_specs=vmem(1)[0],
        compiler_params=pltpu.CompilerParams(vmem_limit_bytes=4 * MIB),
    )(core, mine, theirs)


def first_part(*operands):
    return pl.pallas_call(
        first_kernel,
        out_shape=(
            jax.ShapeDtypeStruct((2, GROUP * RUN, 128), jnp.float32),
            jax.ShapeDtypeStruct((2, GROUP * RUN, 256), jnp.float32),
        ),
        in_specs=vmem(4),
        out_specs=tuple(vmem(2)),
        scratch_shapes=[
            pltpu.VMEM((2, 6, RUN, 256), jnp.bfloat16),
            pltpu.VMEM((6, GROUP * RUN, 256), jnp.float32),
        ],
        compiler_params=pltpu.CompilerParams(vmem_limit_bytes=20 * MIB),
        cost_estimate=pl.CostEstimate(flops=4 << 29, bytes_accessed=8 << 20, transcendentals=2 << 20),
    )(*operands)


def second_part(mine, *operands):
    return pl.pallas_call(
        functools.partial(second_kernel, mine),
        out_shape=jax.ShapeDtypeStruct((RUN, GROUP * 128), jnp.bfloat16),
        in_specs=smem() + vmem(6),
        out_specs=vmem(1)[0],
        scratch_shapes=[
            pltpu.VMEM((1, GROUP * RUN, 128), jnp.float32),
            pltpu.VMEM((GROUP * RUN, 256), jnp.float32),
            pltpu.VMEM((1, 4, RUN, 256), jnp.bfloat16),
            pltpu.VMEM((4, GROUP * RUN, 256), jnp.float32),
        ],
        compiler_params=pltpu.CompilerParams(vmem_limit_bytes=16 * MIB),
        cost_estimate=pl.CostEstimate(flops=2 << 29, bytes_accessed=8 << 20, transcendentals=1 << 20),
    )(*operands)


def body(queries, key_tensor, value_tensor, positions):
    group = ("x", "c")
    packed = pack(positions, key_tensor, value_tensor)
    own = rearrange(
        repack_kernel, lax.all_to_all(packed, group, split_axis=0, concat_axis=0, tiled=True)
    )
    p1 = lax.ppermute(own, AXES, ring_route(4, 0))
    p4 = lax.ppermute(own, AXES, ring_route(5, 1))
    p2 = lax.ppermute(own, AXES, ring_route(1, 1))
    p3 = lax.ppermute(rearrange(relay_kernel, own, p1), AXES, ring_route(2, 2))
    q = lax.all_to_all(
        queries.reshape(ROWS, 8, GROUP * 128), group, split_axis=1, concat_axis=0, tiled=True
    ).reshape(4, 2, ROWS, GROUP * 128)
    m1, acc1 = first_part(q, own, p1, p2)
    core = lax.axis_index("c").astype(jnp.int32).reshape(1)
    rest = (core, q, own, p4, p3, m1, acc1)
    theirs = lax.ppermute(second_part(False, *rest), "c", [(0, 1), (1, 0)])
    block = join(core, second_part(True, *rest), theirs).reshape(4, ROWS, 2 * GROUP * 128)
    result = lax.all_to_all(block, "x", split_axis=0, concat_axis=0, tiled=True)
    return jnp.concatenate([result[x] for x in range(4)], axis=1)


def solution(mesh):
    finer = Mesh(mesh.devices.reshape(SIZES), AXES)
    return jax.shard_map(
        body,
        mesh=finer,
        in_specs=(P(AXES, None), P(AXES, None), P(AXES, None), P(AXES)),
        out_specs=P(AXES, None),
        check_vma=False,
    )
```

```python
import math

import jax
import jax.numpy as jnp
from jax import lax
from jax.experimental import pallas as pl
from jax.experimental.pallas import tpu as pltpu
from jax.sharding import Mesh
from jax.sharding import PartitionSpec as P

HEAD_DIMENSION = 128
RUN = 256
ROWS = 64
FLAG_ROWS = 8
GROUP = 8
SCALE = math.log2(math.e) / math.sqrt(HEAD_DIMENSION)
NEG_BIG = -1e30
AXES = ("yh", "x", "z", "yl", "c")
SIZES = (2, 4, 8, 4, 2)
MIB = 1024 * 1024


def ring_route(shift, back):
    nyh, nx, nz, nyl, nc = SIZES
    route = []
    for yh in range(nyh):
        for x in range(nx):
            for z in range(nz):
                for yl in range(nyl):
                    for c in range(nc):
                        ring = (yh * nyl + yl - shift) % (nyh * nyl)
                        chain = (z * nyl + yl - back) % (nz * nyl)
                        z2, yl2 = divmod(chain, nyl)
                        src = (((ring // nyl * nx + x) * nz + z2) * nyl + yl2) * nc + c
                        dst = (((yh * nx + x) * nz + z) * nyl + yl) * nc + c
                        route.append((src, dst))
    return route


def vmem(count):
    return [pl.BlockSpec(memory_space=pltpu.VMEM)] * count


def smem():
    return [pl.BlockSpec(memory_space=pltpu.SMEM)]


def pack_kernel(pos_ref, k_ref, v_ref, out_ref):
    run = jnp.right_shift(pos_ref[0], 8).astype(jnp.float32)
    flags = jnp.full((FLAG_ROWS, 256), run, jnp.float32).astype(jnp.bfloat16)
    for g in range(8):
        lanes = slice(g * 128, (g + 1) * 128)
        both = jnp.concatenate([k_ref[:, lanes], v_ref[:, lanes]], axis=1)
        out_ref[g] = jnp.concatenate([both, flags], axis=0)


def pack(positions, key_tensor, value_tensor):
    return pl.pallas_call(
        pack_kernel,
        out_shape=jax.ShapeDtypeStruct((8, ROWS + FLAG_ROWS, 256), jnp.bfloat16),
        in_specs=smem() + vmem(2),
        out_specs=vmem(1)[0],
        compiler_params=pltpu.CompilerParams(vmem_limit_bytes=56 * MIB),
    )(positions, key_tensor, value_tensor)


def repack_kernel(in_ref, out_ref, plain_ref):
    flags = []
    for c in range(2):
        for x in range(4):
            block = in_ref[c * 4 + x]
            at = c * RUN + x * ROWS
            out_ref[at : at + ROWS, :] = block[0:ROWS, :]
            plain_ref[at : at + ROWS, :] = block[0:ROWS, :]
        flags.append(block[ROWS : ROWS + FLAG_ROWS, 0:128])
    line = jnp.concatenate(flags, axis=1)
    out_ref[2 * RUN : 2 * RUN + 16, :] = jnp.concatenate([line, line], axis=0)


def relay_kernel(own_ref, other_ref, out_ref):
    last = slice(2 * RUN, 2 * RUN + 16)
    out_ref[0:RUN, :] = own_ref[RUN : 2 * RUN, :]
    out_ref[RUN : 2 * RUN, :] = other_ref[RUN : 2 * RUN, :]
    out_ref[last, 0:128] = own_ref[last, 128:256]
    mirror = 127.0 - own_ref[last, 128:256].astype(jnp.float32)
    out_ref[last, 128:256] = mirror.astype(jnp.bfloat16)


def rearrange(kernel, *operands):
    return pl.pallas_call(
        kernel,
        out_shape=jax.ShapeDtypeStruct((2 * RUN + 16, 256), jnp.bfloat16),
        in_specs=vmem(len(operands)),
        out_specs=vmem(1)[0],
        compiler_params=pltpu.CompilerParams(vmem_limit_bytes=4 * MIB),
    )(*operands)


def repack(block):
    return pl.pallas_call(
        repack_kernel,
        out_shape=tuple(
            jax.ShapeDtypeStruct((2 * RUN + extra, 256), jnp.bfloat16) for extra in (16, 0)
        ),
        in_specs=vmem(1),
        out_specs=tuple(vmem(2)),
        compiler_params=pltpu.CompilerParams(vmem_limit_bytes=4 * MIB),
    )(block)


def flag(ref, half):
    rows = ref.shape[0]
    tile = ref[rows - 16 : rows, half * 128 : (half + 1) * 128].astype(jnp.float32)
    return jnp.max(tile).astype(jnp.int32)


def gather_visible(slots, own_run, kv_ref, i, start):
    count = jnp.int32(start)
    for ref, row, run in slots:
        seen = run < own_run
        at = count

        @pl.when(seen)
        def _(ref=ref, row=row, at=at):
            kv_ref[i, at] = ref[row : row + RUN, :]

        count = count + seen.astype(jnp.int32)
    return count


def lane_fold(s):
    return jnp.maximum(s[:, 0:128], s[:, 128:256])


def scores(q, keys):
    return lax.dot_general(q, keys, (((1,), (1,)), ((), ())), preferred_element_type=jnp.float32)


def queries_of(q_ref, i, h):
    return q_ref[pl.ds(pl.multiple_of(i * RUN, RUN), RUN), h * 128 : (h + 1) * 128]


def head_rows(h):
    return slice(h * RUN, (h + 1) * RUN)


def weighted(s_ref, m_ref, kv_ref, i, at, rows):
    m = m_ref[i, rows, :]
    weights, values = [], []
    for j in at:
        for lanes in (slice(0, 128), slice(128, 256)):
            weights.append(jnp.exp2((s_ref[j, rows, lanes] - m) * SCALE).astype(jnp.bfloat16))
        values.append(kv_ref[i, j, :, 128:256])
    values = jnp.concatenate(values, axis=0)
    values = jnp.concatenate([values, jnp.ones(values.shape, jnp.bfloat16)], axis=1)
    return jnp.dot(jnp.concatenate(weights, axis=1), values, preferred_element_type=jnp.float32)


def row_max(m):
    return jnp.broadcast_to(jnp.max(m, axis=1, keepdims=True), m.shape)


def first_kernel(q_ref, own_ref, other_ref, p2_ref, m_ref, acc_ref, kv_ref, s_ref):
    runs = [flag(own_ref, c) for c in range(2)]
    other = [(other_ref, c * RUN, 127 - runs[c]) for c in range(2)]
    near = [(p2_ref, c * RUN, flag(p2_ref, c)) for c in range(2)]
    slots = [[other[0]] + near, [other[1], (own_ref, 0, runs[0]), other[0]] + near]
    counts = []
    for i in range(2):
        kv_ref[i, 0] = own_ref[i * RUN : (i + 1) * RUN, :]
        counts.append(gather_visible(slots[i], runs[i], kv_ref, i, 1))
    lower = lax.broadcasted_iota(jnp.int32, (RUN, RUN), 0) >= lax.broadcasted_iota(
        jnp.int32, (RUN, RUN), 1
    )

    @pl.loop(0, 2)
    def _(i):
        count = jnp.where(i == 0, counts[0], counts[1])
        for h in range(GROUP):
            s = jnp.where(lower, scores(queries_of(q_ref, i, h), kv_ref[i, 0, :, 0:128]), NEG_BIG)
            s_ref[0, head_rows(h), :] = s
            m_ref[i, head_rows(h), :] = lane_fold(s)

        @pl.loop(1, count)
        def _(j):
            for h in range(GROUP):
                s = scores(queries_of(q_ref, i, h), kv_ref[i, j, :, 0:128])
                s_ref[j, head_rows(h), :] = s
                m_ref[i, head_rows(h), :] = jnp.maximum(m_ref[i, head_rows(h), :], lane_fold(s))

        for h in range(GROUP):
            m_ref[i, head_rows(h), :] = row_max(m_ref[i, head_rows(h), :])
            acc_ref[i, head_rows(h), :] = weighted(s_ref, m_ref, kv_ref, i, [0], head_rows(h))

        @pl.loop(1, count)
        def _(j):
            for h in range(GROUP):
                acc_ref[i, head_rows(h), :] = acc_ref[i, head_rows(h), :] + weighted(
                    s_ref, m_ref, kv_ref, i, [j], head_rows(h)
                )


def second_kernel(
    q_ref, own_ref, p2_ref, p4_ref, p3_ref, m1_ref, acc1_ref, out_ref, m_ref, acc_ref, kv_ref, s_ref
):
    runs = [flag(own_ref, c) for c in range(2)]
    near = [(p4_ref, c * RUN, 127 - flag(p2_ref, c)) for c in range(2)]
    far = [(p3_ref, c * RUN, flag(p3_ref, c)) for c in range(2)]
    slots = [near + far, near]
    counts = [gather_visible(slots[i], runs[i], kv_ref, i, 0) for i in range(2)]

    @pl.loop(0, 2)
    def _(i):
        count = jnp.where(i == 0, counts[0], counts[1])
        for h in range(GROUP):
            m_ref[i, head_rows(h), :] = m1_ref[i, head_rows(h), :]

        @pl.loop(0, count)
        def _(j):
            for h in range(GROUP):
                s = scores(queries_of(q_ref, i, h), kv_ref[i, j, :, 0:128])
                s_ref[j, head_rows(h), :] = s
                m_ref[i, head_rows(h), :] = jnp.maximum(m_ref[i, head_rows(h), :], lane_fold(s))

        for h in range(GROUP):
            m = row_max(m_ref[i, head_rows(h), :])
            m_ref[i, head_rows(h), :] = m
            rescale = jnp.exp2((m1_ref[i, head_rows(h), :] - m) * SCALE)
            for lanes in (slice(0, 128), slice(128, 256)):
                acc_ref[head_rows(h), lanes] = acc1_ref[i, head_rows(h), lanes] * rescale
        odd = count % 2

        @pl.when(odd == 1)
        def _():
            for h in range(GROUP):
                acc_ref[head_rows(h), :] = acc_ref[head_rows(h), :] + weighted(
                    s_ref, m_ref, kv_ref, i, [0], head_rows(h)
                )

        @pl.loop(0, count // 2)
        def _(pair):
            j = odd + 2 * pair
            for h in range(GROUP):
                acc_ref[head_rows(h), :] = acc_ref[head_rows(h), :] + weighted(
                    s_ref, m_ref, kv_ref, i, [j, j + 1], head_rows(h)
                )

        at = pl.ds(pl.multiple_of(i * RUN, RUN), RUN)
        for h in range(GROUP):
            block = acc_ref[head_rows(h), :]
            out_ref[at, h * 128 : (h + 1) * 128] = (block[:, 0:128] / block[:, 128:256]).astype(
                jnp.bfloat16
            )


def first_part(*operands):
    return pl.pallas_call(
        first_kernel,
        out_shape=(
            jax.ShapeDtypeStruct((2, GROUP * RUN, 128), jnp.float32),
            jax.ShapeDtypeStruct((2, GROUP * RUN, 256), jnp.float32),
        ),
        in_specs=vmem(4),
        out_specs=tuple(vmem(2)),
        scratch_shapes=[
            pltpu.VMEM((2, 6, RUN, 256), jnp.bfloat16),
            pltpu.VMEM((6, GROUP * RUN, 256), jnp.float32),
        ],
        compiler_params=pltpu.CompilerParams(vmem_limit_bytes=20 * MIB),
        cost_estimate=pl.CostEstimate(flops=4 << 29, bytes_accessed=8 << 20, transcendentals=2 << 20),
    )(*operands)


def second_part(*operands):
    return pl.pallas_call(
        second_kernel,
        out_shape=jax.ShapeDtypeStruct((2 * RUN, GROUP * 128), jnp.bfloat16),
        in_specs=vmem(7),
        out_specs=vmem(1)[0],
        scratch_shapes=[
            pltpu.VMEM((2, GROUP * RUN, 128), jnp.float32),
            pltpu.VMEM((GROUP * RUN, 256), jnp.float32),
            pltpu.VMEM((2, 4, RUN, 256), jnp.bfloat16),
            pltpu.VMEM((4, GROUP * RUN, 256), jnp.float32),
        ],
        compiler_params=pltpu.CompilerParams(vmem_limit_bytes=22 * MIB),
        cost_estimate=pl.CostEstimate(flops=4 << 29, bytes_accessed=8 << 20, transcendentals=2 << 20),
    )(*operands)


def body(queries, key_tensor, value_tensor, positions):
    group = ("c", "x")
    packed = pack(positions, key_tensor, value_tensor)
    own, plain = repack(
        lax.all_to_all(packed, group, split_axis=0, concat_axis=0, tiled=True)
    )
    p1 = lax.ppermute(plain, AXES, ring_route(4, 0))
    p4 = lax.ppermute(plain, AXES, ring_route(5, 1))
    p2 = lax.ppermute(own, AXES, ring_route(1, 1))
    p3 = lax.ppermute(rearrange(relay_kernel, own, p1), AXES, ring_route(2, 2))
    q = lax.all_to_all(
        queries.reshape(ROWS, 8, GROUP * 128), group, split_axis=1, concat_axis=0, tiled=True
    ).reshape(2 * RUN, GROUP * 128)
    m1, acc1 = first_part(q, own, p1, p2)
    out = second_part(q, own, p2, p4, p3, m1, acc1)
    result = lax.all_to_all(
        out.reshape(8, ROWS, GROUP * 128), group, split_axis=0, concat_axis=2, tiled=True
    )
    return result.reshape(ROWS, 8 * GROUP * 128)


def solution(mesh):
    finer = Mesh(mesh.devices.reshape(SIZES), AXES)
    return jax.shard_map(
        body,
        mesh=finer,
        in_specs=(P(AXES, None), P(AXES, None), P(AXES, None), P(AXES)),
        out_specs=P(AXES, None),
        check_vma=False,
    )
```
